128 devices in a mesh: box: 4 (over x_hi, core), cone: 32 (over x_lo, y, z).
Axes of the slice: x: 4 (x_hi: 2, x_lo: 2; x = x_hi * 2 + x_lo), y: 4, z: 4, core: 2. Of those that a mesh axis runs over, the one named last changes fastest.
Arguments:
- fine_values: bfloat16 [2, 2097152, 256], P(None, ('box', 'cone')), may hold values from -6 to 6
- present: int32 [262144, 8], P(('box', 'cone')), may hold values 0 or 1
- mask_one: int32 [262144, 16], P(('box', 'cone')), may hold values 0 or 1
- mask_two: int32 [32768, 64], P(('box', 'cone')), may hold values 0 or 1
- mask_top: int32 [4096, 256], replicated, may hold values 0 or 1
- interp_one: bfloat16 [8, 4, 64, 64], replicated, may hold values from -0.25 to 0.25
- interp_two: bfloat16 [8, 4, 64, 64], replicated, may hold values from -0.25 to 0.25
- interp_top: bfloat16 [8, 4, 64, 64], replicated, may hold values from -0.25 to 0.25
- factor_one: float32 [2, 8, 4, 4, 64], replicated, may hold values from -4 to 4
- factor_two: float32 [2, 8, 16, 4, 64], replicated, may hold values from -4 to 4
- factor_top: float32 [2, 8, 64, 4, 64], replicated, may hold values from -4 to 4
- cone_order: int32 [64], replicated, may hold values from 0 to 63, each once
Outputs:
- top_values: float32 [2, 4096, 16384], P(None, None, ('box', 'cone'))
The draws below stay inside these ranges and needn't reach their ends.
Inputs may be any that keep to these rules, and one draw needn't show every extreme that they name: present and the masks hold 0 or 1. `cone_order`: a permutation of the 64 level-two cones.
All inputs are finite; a program needn't handle non-finite values. No bound on the sum of `present` or of `mask_one` or of `mask_two` on one device may be relied on, other than what follows from the above.
Results may differ from the reference program's by a relative error of at most 0.0064.
Values may be sent and summed in bfloat16 or wider, within the bound.
A program may use at most 256 MiB of HBM per device.

```python
import jax
import jax.numpy as jnp
from jax import lax

NP = 64
Q0 = 4
Q1 = 16
Q2 = 64
Q3 = 256
B3 = 4096
B2 = 32768
B1 = 262144
B0 = 2097152


def with_ends(values, rng, low, top_value):
    index_at = [jax.random.randint(jax.random.fold_in(rng, axis), (), 0, length) for axis, length in enumerate(values.shape)]
    longest = values.shape.index(max(values.shape))
    next_to = index_at[:longest] + [(index_at[longest] + 1) % values.shape[longest]] + index_at[longest + 1:]
    return values.at[tuple(index_at)].set(low).at[tuple(next_to)].set(top_value)


def block_levels(stream_key, shape, pieces, low, top_value):
    level, own = 1.0, jax.random.fold_in(stream_key, 6)
    for position, shards_of in pieces:
        draws = jnp.exp(jax.random.uniform(jax.random.fold_in(own, position), (shards_of,), jnp.float32, low / len(pieces), top_value / len(pieces)))
        level = level * jnp.repeat(draws, shape[position] // shards_of).reshape([-1 if axis == position else 1 for axis in range(len(shape))])
    return level


def centred(key, shape, width, reach, split=(), held_as=jnp.bfloat16):
    array = width * jax.random.normal(key, shape, jnp.float32)
    if split:
        array = array * block_levels(key, shape, split, -0.22, 0.18)
    return jnp.clip(array, -reach, reach).astype(held_as)


def setup_inputs(seed: int = 0) -> dict:
    seeds = jax.random.split(jax.random.key(seed), 13)
    return {
        "fine_values": centred(seeds[0], (2, B0, Q0 * NP), 1.0, 6.0, ((1, 128),)),
        "present": with_ends((jax.random.randint(seeds[1], (B1, 8), 0, 8) < 7).astype(jnp.int32), jax.random.fold_in(seeds[1], 1), 0, 1),
        "mask_one": with_ends((jax.random.randint(seeds[2], (B1, Q1), 0, 4) < 3).astype(jnp.int32), jax.random.fold_in(seeds[2], 1), 0, 1),
        "mask_two": with_ends((jax.random.randint(seeds[3], (B2, Q2), 0, 4) < 3).astype(jnp.int32), jax.random.fold_in(seeds[3], 1), 0, 1),
        "mask_top": with_ends((jax.random.randint(seeds[4], (B3, Q3), 0, 4) < 3).astype(jnp.int32), jax.random.fold_in(seeds[4], 1), 0, 1),
        "interp_one": centred(seeds[5], (8, 4, NP, NP), (8 * NP) ** -0.5, 0.25),
        "interp_two": centred(seeds[6], (8, 4, NP, NP), (8 * NP) ** -0.5, 0.25),
        "interp_top": centred(seeds[7], (8, 4, NP, NP), (8 * NP) ** -0.5, 0.25),
        "factor_one": centred(seeds[8], (2, 8, Q0, 4, NP), 0.7, 4.0, (), jnp.float32),
        "factor_two": centred(seeds[9], (2, 8, Q1, 4, NP), 0.7, 4.0, (), jnp.float32),
        "factor_top": centred(seeds[10], (2, 8, Q2, 4, NP), 0.7, 4.0, (), jnp.float32),
        "cone_order": jax.random.permutation(seeds[11], Q2).astype(jnp.int32),
    }


def kernel(interp, factor):
    weights = interp.astype(jnp.float32)[:, None]
    real_part = factor[0][..., None] * weights
    imag_part = factor[1][..., None] * weights
    stacked = jnp.stack([jnp.stack([real_part, imag_part]), jnp.stack([-imag_part, real_part])])
    return jnp.transpose(stacked, (3, 0, 2, 6, 1, 4, 5)).astype(jnp.bfloat16)


def ascend(children, matrices):
    parents = children.shape[1] // 8
    cones = matrices.shape[0]
    blocks = children.reshape(2, parents, 8, cones, NP)

    def single(cone):
        picked = lax.dynamic_index_in_dim(blocks, cone, 3, False).astype(jnp.float32)
        table = lax.dynamic_index_in_dim(matrices, cone, 0, False).astype(jnp.float32)
        return jnp.einsum('rpjq,rjqzsx->zpsx', picked, table)

    result = lax.map(single, jnp.arange(cones).astype(jnp.int32))
    return jnp.transpose(result, (1, 2, 0, 3, 4))


def masked_level(children, interp, factor, masks):
    result = ascend(children, kernel(interp, factor))
    parents, cones = result.shape[1], result.shape[2]
    result = result * masks.reshape(parents, cones, 4)[None, :, :, :, None].astype(jnp.float32)
    return result.astype(jnp.bfloat16).reshape(2, parents, cones * 4 * NP)


def reference(fine_values, present, mask_one, mask_two, mask_top, interp_one, interp_two, interp_top, factor_one, factor_two, factor_top, cone_order):
    children = fine_values * present.reshape(-1)[None, :, None].astype(jnp.bfloat16)
    level_one = masked_level(children, interp_one, factor_one, mask_one)
    level_two = masked_level(level_one, interp_two, factor_two, mask_two)
    ordered = jnp.take(level_two.reshape(2, B2, Q2, NP), cone_order, axis=2).reshape(2, B2, Q2 * NP)
    top_level = ascend(ordered, kernel(interp_top, jnp.take(factor_top, cone_order, axis=2)))
    masks = jnp.take(mask_top.reshape(B3, Q2, 4), cone_order, axis=1).astype(jnp.float32)
    top_level = top_level * masks[None, :, :, :, None]
    return jnp.transpose(top_level, (0, 1, 3, 2, 4)).reshape(2, B3, Q3 * NP)
```

```python
import functools

import jax
import jax.numpy as jnp
from jax import lax
from jax.experimental import pallas as pl
from jax.experimental.pallas import tpu as pltpu
from jax.sharding import PartitionSpec as P

F32 = jnp.float32
BF16 = jnp.bfloat16
MESH = pl.DeviceIdType.MESH

DEVICES = 128
B1 = 2048
CHUNKS = 4
BLOCK = 256
BLOCKS = B1 // BLOCK
PER_CHUNK = BLOCKS // CHUNKS
QUARTER = BLOCK // 4
N2 = B1 // 8 // CHUNKS
N3 = N2 // 8
ROWS3 = 2 * N3


def offsets():
    every = [
        (x, y, z, core) for x in range(4) for y in range(4) for z in range(4) for core in range(2)
    ][1:]
    hops = lambda o: sum(min(v, 4 - v) for v in o[:3])
    order = sorted(range(127), key=lambda i: (i * 77 + 31) % 127)
    return sorted([every[i] for i in order], key=lambda o: -hops(o))


def target(offset):
    box, cone = lax.axis_index("box"), lax.axis_index("cone")
    x = (box // 2) * 2 + cone // 16
    x = (x + offset[0]) % 4
    y = (cone // 4 + offset[1]) % 4
    z = (cone + offset[2]) % 4
    core = (box + offset[3]) % 2
    return (x // 2) * 2 + core, (x % 2) * 16 + y * 4 + z


def prepare_factor(f_ref, scratch, cones):
    for rj in range(16):
        parts = [f_ref[pl.ds(rj * cones * 4 + s, cones, stride=4), :] for s in range(4)]
        scratch[rj] = jnp.concatenate(parts, axis=1)


def prepare_weights(w_ref, scratch):
    row = lax.broadcasted_iota(jnp.int32, (64, 64), 0)
    column = lax.broadcasted_iota(jnp.int32, (64, 64), 1)
    eye = (row == column).astype(BF16)
    for j in range(8):
        scratch[j] = lax.dot_general(
            eye, w_ref[j], (((1,), (1,)), ((), ())), preferred_element_type=F32
        )


def kernel(
    fine, present, mask_one, mask_two, mask_top, w_one, w_two, w_top, f_one, f_two, f_top, order,
    received,
    fine_buf, split, lhs_a, lhs_b, k_one, out_one, lhs_two, k_two, out_two, lhs_top, w_block,
    present_t, mask_one_t, mask_two_t, mask_rows, mask_top_x, wt, fs_one, fs_two, fs_top,
    top_out, send_buf,
    fine_sem, mask_sem, send_sem, recv_sem, local_sem,
):
    box, cone_index = lax.axis_index("box"), lax.axis_index("cone")
    me = box * 32 + cone_index
    low_lane = lambda rows: lax.broadcasted_iota(jnp.int32, (rows, 128), 1) < 64

    def fetch(block, slot):
        return pltpu.make_async_copy(
            fine.at[:, pl.ds(block * (BLOCK * 8), BLOCK * 8), :], fine_buf.at[slot], fine_sem.at[slot]
        )

    fetch(0, 0).start()
    fetch(1, 1).start()
    rows_copy = pltpu.make_async_copy(mask_top.at[pl.ds(me * 32, 32)], mask_rows, mask_sem)
    rows_copy.start()

    barrier = pltpu.get_barrier_semaphore()
    for offset in offsets():
        pl.semaphore_signal(barrier, inc=1, device_id=target(offset), device_id_type=MESH)

    for i in range(B1 // 256):
        at = pl.ds(i * 256, 256)
        present_t[at, :] = present[:, at].astype(F32).T
        mask_one_t[at, :] = mask_one[:, at].astype(F32).T
    mask_two_t[...] = mask_two[...].astype(F32).T
    prepare_factor(f_one, fs_one, 4)
    prepare_factor(f_two, fs_two, 16)
    prepare_factor(f_top, fs_top, 64)

    prepare_weights(w_one, wt)
    for c in range(4):
        for j in range(8):
            at = (j ^ (c % 2)) * 64
            real = fs_one[j, c : c + 1, :] * wt[j]
            imag = fs_one[8 + j, c : c + 1, :] * wt[j]
            k_one[c, at : at + 64, 0:256] = real.astype(BF16)
            k_one[c, at : at + 64, 256:512] = imag.astype(BF16)
            k_one[c, 512 + at : 576 + at, 0:256] = (-imag).astype(BF16)
            k_one[c, 512 + at : 576 + at, 256:512] = real.astype(BF16)

    prepare_weights(w_two, wt)

    @pl.loop(0, 8)
    def _(pair):
        for odd in range(2):
            c = pair * 2 + odd
            for j in range(8):
                at = (j ^ odd) * 64
                k_two[c, at : at + 64, :] = (fs_two[j, pl.ds(c, 1), :] * wt[j]).astype(BF16)
                k_two[c, 512 + at : 576 + at, :] = (fs_two[8 + j, pl.ds(c, 1), :] * wt[j]).astype(BF16)

    prepare_weights(w_top, wt)
    for j in range(8):
        zero = jnp.zeros((64, 256), BF16)
        w_block[0, j, 0:64, :] = wt[j].astype(BF16)
        w_block[0, j, 64:128, :] = zero
        w_block[1, j, 0:64, :] = zero
        w_block[1, j, 64:128, :] = wt[j].astype(BF16)

    rows_copy.wait()
    for i in range(CHUNKS):
        rows = mask_rows[i * N3 : (i + 1) * N3, :].astype(F32)
        for c in range(64):
            for t in range(2):
                at = 4 * c + 2 * t
                mask_top_x[i * 64 + c, :, t * 128 : t * 128 + 128] = jnp.where(
                    low_lane(N3), rows[:, at : at + 1], rows[:, at + 1 : at + 2]
                )

    def relay(slot, block, quarter, lhs):
        low = low_lane(QUARTER)
        for r in range(2):
            for t in range(2):
                split[r, t] = fine_buf[
                    slot, r, pl.ds(quarter * QUARTER * 8, QUARTER * 8), t * 128 : t * 128 + 128
                ].astype(F32)
        here = present_t[pl.ds(block * BLOCK + quarter * QUARTER, QUARTER), :]
        rows = slice(quarter * QUARTER, quarter * QUARTER + QUARTER)
        for m in range(4):
            first = jnp.broadcast_to(here[:, 2 * m : 2 * m + 1], (QUARTER, 128))
            second = jnp.broadcast_to(here[:, 2 * m + 1 : 2 * m + 2], (QUARTER, 128))
            for r in range(2):
                lanes = slice(r * 512 + m * 128, r * 512 + m * 128 + 128)
                for t in range(2):
                    a = split[r, t, pl.ds(2 * m, QUARTER, stride=8), :] * first
                    b = split[r, t, pl.ds(2 * m + 1, QUARTER, stride=8), :] * second
                    b = pltpu.roll(b, 64, 1)
                    lhs[2 * t, rows, lanes] = jnp.where(low, a, b).astype(BF16)
                    lhs[2 * t + 1, rows, lanes] = jnp.where(low, b, a).astype(BF16)

    fetch(0, 0).wait()
    for quarter in range(4):
        relay(0, 0, quarter, lhs_a)
    pl.semaphore_wait(barrier, DEVICES - 1)

    @pl.loop(0, CHUNKS)
    def _(chunk):
        for k in range(PER_CHUNK):
            block = chunk * PER_CHUNK + k
            now, later = (lhs_a, lhs_b) if k % 2 == 0 else (lhs_b, lhs_a)

            @pl.when(block + 1 < BLOCKS)
            def _():
                fetch(block + 1, (k + 1) % 2).wait()

            @pl.when(block + 2 < BLOCKS)
            def _():
                fetch(block + 2, k % 2).start()

            next_block = (block + 1) % BLOCKS
            low = low_lane(32)
            for c in range(4):
                result = jnp.dot(now[c], k_one[c], preferred_element_type=F32)
                masks = mask_one_t[pl.ds(block * BLOCK, BLOCK), :]
                for t in range(2):
                    at = 4 * c + 2 * t
                    mask = jnp.where(low_lane(BLOCK), masks[:, at : at + 1], masks[:, at + 1 : at + 2])
                    for z in range(2):
                        out_one[z, t] = result[:, z * 256 + t * 128 : z * 256 + t * 128 + 128] * mask
                relay((k + 1) % 2, next_block, c, later)
                for z in range(2):
                    rows = slice(z * N2 + k * 32, z * N2 + k * 32 + 32)
                    other = slice((1 - z) * N2 + k * 32, (1 - z) * N2 + k * 32 + 32)
                    for m in range(4):
                        lanes = slice(m * 128, m * 128 + 128)
                        lanes_other = slice(512 + m * 128, 640 + m * 128)
                        for t in range(2):
                            a = out_one[z, t, pl.ds(2 * m, 32, stride=8), :]
                            b = pltpu.roll(out_one[z, t, pl.ds(2 * m + 1, 32, stride=8), :], 64, 1)
                            even, odd = jnp.where(low, a, b), jnp.where(low, b, a)
                            lhs_two[4 * c + 2 * t, rows, lanes] = even.astype(BF16)
                            lhs_two[4 * c + 2 * t + 1, rows, lanes] = odd.astype(BF16)
                            if z == 1:
                                even, odd = -even, -odd
                            lhs_two[4 * c + 2 * t, other, lanes_other] = even.astype(BF16)
                            lhs_two[4 * c + 2 * t + 1, other, lanes_other] = odd.astype(BF16)

        for c in range(16):
            result = jnp.dot(lhs_two[c], k_two[c], preferred_element_type=F32)
            masks = mask_two_t[pl.ds(chunk * N2, N2), :]
            for t in range(2):
                at = 4 * c + 2 * t
                mask = jnp.where(low_lane(N2), masks[:, at : at + 1], masks[:, at + 1 : at + 2])
                for z in range(2):
                    out_two[c % 2, t, z * N2 : (z + 1) * N2, :] = (
                        result[z * N2 : (z + 1) * N2, t * 128 : t * 128 + 128] * mask
                    )
            for j in range(8):
                for t in range(2):
                    lhs_top[j, c * ROWS3 : (c + 1) * ROWS3, t * 128 : t * 128 + 128] = out_two[
                        c % 2, t, pl.ds(j, ROWS3, stride=8), :
                    ].astype(BF16)

        group = 8

        @pl.loop(0, 4 * (16 // group))
        def _(step):
            s = step % 4
            first = (step // 4) * group
            half = pl.multiple_of((s // 2) * 128, 128)
            real = [None] * group
            imag = [None] * group
            for j in range(8):
                part = jnp.dot(
                    lhs_top[j, pl.ds(pl.multiple_of(first * ROWS3, group * ROWS3), group * ROWS3), pl.ds(half, 128)],
                    w_block[s % 2, j],
                    preferred_element_type=F32,
                )
                for g in range(group):
                    re = part[g * ROWS3 : g * ROWS3 + N3]
                    im = part[g * ROWS3 + N3 : (g + 1) * ROWS3]
                    c = 4 * (first + g) + s
                    f0 = fs_top[j, pl.ds(c, 1), :]
                    f1 = fs_top[8 + j, pl.ds(c, 1), :]
                    new_re = f0 * re - f1 * im
                    new_im = f1 * re + f0 * im
                    real[g] = new_re if j == 0 else real[g] + new_re
                    imag[g] = new_im if j == 0 else imag[g] + new_im
            for g in range(group):
                c = 4 * (first + g) + s
                mask = mask_top_x[chunk * 64 + c]
                top_out[c, 0:N3, :] = real[g] * mask
                top_out[c, N3:ROWS3, :] = imag[g] * mask

        @pl.loop(0, 32)
        def _(i):
            low = low_lane(ROWS3)
            c0, c1 = order[2 * i], order[2 * i + 1]
            for t in range(2):
                a = top_out[c0, :, t * 128 : t * 128 + 128]
                b = top_out[c1, :, t * 128 : t * 128 + 128]
                send_buf[chunk, 2 * t * 32 + i] = jnp.where(low, a, pltpu.roll(b, 64, 1)).astype(BF16)
                send_buf[chunk, (2 * t + 1) * 32 + i] = jnp.where(low, pltpu.roll(a, 64, 1), b).astype(BF16)

        pltpu.make_async_copy(send_buf.at[chunk, me], received.at[chunk, me], local_sem).start()
        for offset in offsets():
            to_box, to_cone = target(offset)
            pltpu.make_async_remote_copy(
                src_ref=send_buf.at[chunk, to_box * 32 + to_cone],
                dst_ref=received.at[chunk, me],
                send_sem=send_sem,
                recv_sem=recv_sem,
                device_id=(to_box, to_cone),
                device_id_type=MESH,
            ).start()

    whole = send_buf.at[:, pl.ds(0, DEVICES - 1)]
    pltpu.make_async_copy(send_buf.at[:, 0], send_buf.at[:, 0], local_sem).wait()
    pltpu.make_async_copy(whole, whole, send_sem).wait()
    pltpu.make_async_copy(whole, whole, recv_sem).wait()


def on_device(
    fine_values, present, mask_one, mask_two, mask_top,
    interp_one, interp_two, interp_top, factor_one, factor_two, factor_top, cone_order,
):
    vmem = pl.BlockSpec(memory_space=pltpu.VMEM)
    hbm = pl.BlockSpec(memory_space=pl.ANY)
    received = pl.pallas_call(
        kernel,
        out_shape=jax.ShapeDtypeStruct((CHUNKS, DEVICES, ROWS3, 128), BF16),
        in_specs=[hbm, vmem, vmem, vmem, hbm] + [vmem] * 6 + [pl.BlockSpec(memory_space=pltpu.SMEM)],
        out_specs=hbm,
        scratch_shapes=[
            pltpu.VMEM((2, 2, BLOCK * 8, 256), BF16),
            pltpu.VMEM((2, 2, QUARTER * 8, 128), F32),
            pltpu.VMEM((4, BLOCK, 1024), BF16),
            pltpu.VMEM((4, BLOCK, 1024), BF16),
            pltpu.VMEM((4, 1024, 512), BF16),
            pltpu.VMEM((2, 2, BLOCK, 128), F32),
            pltpu.VMEM((16, 2 * N2, 1024), BF16),
            pltpu.VMEM((16, 1024, 256), BF16),
            pltpu.VMEM((2, 2, 2 * N2, 128), F32),
            pltpu.VMEM((8, 16 * ROWS3, 256), BF16),
            pltpu.VMEM((2, 8, 128, 256), BF16),
            pltpu.VMEM((B1, 8), F32),
            pltpu.VMEM((B1, 16), F32),
            pltpu.VMEM((B1 // 8, 64), F32),
            pltpu.VMEM((32, 256), jnp.int32),
            pltpu.VMEM((CHUNKS * 64, N3, 256), F32),
            pltpu.VMEM((8, 64, 256), F32),
            pltpu.VMEM((16, 4, 256), F32),
            pltpu.VMEM((16, 16, 256), F32),
            pltpu.VMEM((16, 64, 256), F32),
            pltpu.VMEM((64, ROWS3, 256), F32),
            pltpu.VMEM((CHUNKS, DEVICES, ROWS3, 128), BF16),
            pltpu.SemaphoreType.DMA((2,)),
            pltpu.SemaphoreType.DMA,
            pltpu.SemaphoreType.DMA,
            pltpu.SemaphoreType.DMA,
            pltpu.SemaphoreType.DMA,
        ],
        compiler_params=pltpu.CompilerParams(
            collective_id=0, has_side_effects=True, vmem_limit_bytes=60 << 20
        ),
        name="levels",
    )(
        fine_values,
        present.T,
        mask_one.T,
        mask_two.T,
        mask_top,
        interp_one.reshape(8, 256, 64),
        interp_two.reshape(8, 256, 64),
        interp_top.reshape(8, 256, 64),
        factor_one.reshape(-1, 64),
        factor_two.reshape(-1, 64),
        factor_top.reshape(-1, 64),
        cone_order,
    )
    top = received.reshape(CHUNKS, DEVICES, 2, N3, 128)
    return jnp.transpose(top, (2, 1, 0, 3, 4)).reshape(2, DEVICES * 32, 128).astype(F32)


def solution(mesh):
    split = P(("box", "cone"), None)
    in_specs = (P(None, ("box", "cone"), None), split, split, split) + (P(),) * 8
    return jax.shard_map(
        on_device,
        mesh=mesh,
        in_specs=in_specs,
        out_specs=P(None, None, ("box", "cone")),
        check_vma=False,
    )
```

```python
import functools

import jax
import jax.numpy as jnp
from jax import lax
from jax.experimental import pallas as pl
from jax.experimental.pallas import tpu as pltpu
from jax.sharding import PartitionSpec as P

F32 = jnp.float32
BF16 = jnp.bfloat16
MESH = pl.DeviceIdType.MESH

DEVICES = 128
B1 = 2048
CHUNKS = 4
BLOCK = B1 // CHUNKS
N2 = BLOCK // 8
N3 = N2 // 8
ROWS3 = 2 * N3


def offsets():
    every = [
        (x, y, z, core) for x in range(4) for y in range(4) for z in range(4) for core in range(2)
    ][1:]
    hops = lambda o: sum(min(v, 4 - v) for v in o[:3])
    order = sorted(range(127), key=lambda i: (i * 77 + 31) % 127)
    return sorted([every[i] for i in order], key=lambda o: -hops(o))


def prepare_factor(f_ref, scratch, cones):
    for rj in range(16):
        parts = [f_ref[pl.ds(rj * cones * 4 + s, cones, stride=4), :] for s in range(4)]
        scratch[rj] = jnp.concatenate(parts, axis=1)


def prepare_weights(w_ref, scratch):
    row = lax.broadcasted_iota(jnp.int32, (64, 64), 0)
    column = lax.broadcasted_iota(jnp.int32, (64, 64), 1)
    eye = (row == column).astype(BF16)
    for j in range(8):
        scratch[j] = lax.dot_general(
            eye, w_ref[j], (((1,), (1,)), ((), ())), preferred_element_type=F32
        )


def spread(rows, columns, width, first):
    row = lax.broadcasted_iota(jnp.int32, (rows, columns), 0)
    column = lax.broadcasted_iota(jnp.int32, (rows, columns), 1)
    return (row == first + column // width).astype(BF16)


def kernel(
    fine, mask_top, *refs,
):
    small, (order, received), buffers, refs = refs[:9], refs[9:11], refs[11:20], refs[20:]
    present, mask_one, w_one, f_one, mask_two, w_two, f_two, w_top, f_top = buffers
    (
    fine_buf, here, lhs_one, k_one, lhs_two, k_two, lhs_top, w_block, gather,
    present_t, mask_one_t, mask_two_t, spread_present, spread_one, spread_two, spread_top,
    mask_rows, mask_top_x, wt, fs_one, fs_two, fs_top, top_out, send_buf,
    fine_sem, mask_sem, send_sem, recv_sem, local_sem, small_sem,
    ) = refs
    box, cone_index = lax.axis_index("box"), lax.axis_index("cone")
    me = box * 32 + cone_index
    low_lane = lambda rows: lax.broadcasted_iota(jnp.int32, (rows, 128), 1) < 64

    def fetch(chunk, slot):
        part = BLOCK * 8 // 4
        for r in range(2):
            for i in range(4):
                pltpu.make_async_copy(
                    fine.at[r, pl.ds(chunk * (BLOCK * 8) + i * part, part), :],
                    fine_buf.at[slot, r, pl.ds(i * part, part), :],
                    fine_sem.at[slot],
                ).start()

    def fetched(slot):
        pltpu.make_async_copy(fine_buf.at[slot], fine_buf.at[slot], fine_sem.at[slot]).wait()

    fetch(0, 0)
    copies = [pltpu.make_async_copy(a, b, small_sem.at[i]) for i, (a, b) in enumerate(zip(small, buffers))]
    for copy in copies:
        copy.start()
    rows_copy = pltpu.make_async_copy(mask_top.at[pl.ds(me * 32, 32)], mask_rows, mask_sem)
    rows_copy.start()
    fetch(1, 1)

    x, y, z, core = (box // 2) * 2 + cone_index // 16, cone_index // 4 % 4, cone_index % 4, box % 2
    xs = [(x + i) % 4 for i in range(4)]
    to_x = [(v // 2 * 2, v % 2 * 16) for v in xs]
    to_y = [(y + i) % 4 * 4 for i in range(4)]
    to_z = [(z + i) % 4 for i in range(4)]
    to_core = [core, 1 - core]

    def target(offset):
        to_box, to_cone = to_x[offset[0]]
        return to_box + to_core[offset[3]], to_cone + to_y[offset[1]] + to_z[offset[2]]

    barrier = pltpu.get_barrier_semaphore()
    for offset in offsets():
        pl.semaphore_signal(barrier, inc=1, device_id=target(offset), device_id_type=MESH)

    row = lax.broadcasted_iota(jnp.int32, (256, 256), 0)
    column = lax.broadcasted_iota(jnp.int32, (256, 256), 1)
    gather[...] = (column == (row % 8) * 32 + (row // 8) % 4 * 8 + row // 32).astype(BF16)
    row = lax.broadcasted_iota(jnp.int32, (BLOCK, BLOCK), 0)
    column = lax.broadcasted_iota(jnp.int32, (BLOCK, BLOCK), 1)
    reorder_one = (column == (row % 8) * 64 + (row // 8) % 8 * 8 + row // 64).astype(BF16)
    row = lax.broadcasted_iota(jnp.int32, (N2, N2), 0)
    column = lax.broadcasted_iota(jnp.int32, (N2, N2), 1)
    reorder_two = (column == (row % 8) * 8 + row // 8).astype(BF16)
    turned = lambda order, mask: lax.dot_general(
        order, mask.astype(F32).astype(BF16), (((1,), (1,)), ((), ())), preferred_element_type=F32
    ).astype(BF16)
    copies[0].wait()
    copies[1].wait()
    copies[4].wait()
    for i in range(CHUNKS):
        at = slice(i * BLOCK, (i + 1) * BLOCK)
        present_t[at, :] = turned(reorder_one, present[:, at])
        mask_one_t[at, :] = turned(reorder_one, mask_one[:, at])
        at = slice(i * N2, (i + 1) * N2)
        mask_two_t[at, :] = turned(reorder_two, mask_two[:, at])
    spread_present[...] = spread(8, 1024, 128, 0)
    for c in range(4):
        spread_one[c] = spread(16, 256, 64, 4 * c)
    for c in range(16):
        spread_two[c] = spread(64, 256, 64, 4 * c)
    spread_top[...] = spread(16, 1024, 64, 0)
    def relay(slot, chunk):
        low = low_lane(16)
        for half in range(2):
            at = pl.ds(chunk * BLOCK + half * 256, 256)
            here[half] = jnp.dot(present_t[at, :], spread_present[...], preferred_element_type=F32)
            for pair in range(4):
                for r in range(2):
                    picked = []
                    for j2 in (2 * pair, 2 * pair + 1):
                        rows = [
                            fine_buf[slot, r, (8 * p + j2) * 64 + half * 32 : (8 * p + j2) * 64 + half * 32 + 32, :]
                            for p in range(8)
                        ]
                        picked.append(
                            jnp.dot(gather[...], jnp.concatenate(rows, axis=0), preferred_element_type=F32)
                        )
                    for j1 in range(4):
                        at = j1 * 64 + pair * 16
                        to = half * 256 + at
                        for m in range(4):
                            lanes = slice(r * 512 + m * 128, r * 512 + m * 128 + 128)
                            for t in range(2):
                                a, b = [
                                    jnp.concatenate(
                                        [
                                            part[j * 32 + j1 * 8 : j * 32 + j1 * 8 + 8, t * 128 : t * 128 + 128]
                                            for part in picked
                                        ],
                                        axis=0,
                                    )
                                    * here[half, at : at + 16, j * 128 : j * 128 + 128]
                                    for j in (2 * m, 2 * m + 1)
                                ]
                                b = pltpu.roll(b, 64, 1)
                                lhs_one[2 * t, to : to + 16, lanes] = jnp.where(low, a, b).astype(BF16)
                                lhs_one[2 * t + 1, to : to + 16, lanes] = jnp.where(low, b, a).astype(BF16)

    fetched(0)
    relay(0, 0)
    fetch(2, 0)

    for i in (2, 3, 5, 6, 7, 8):
        copies[i].wait()
    prepare_factor(f_one, fs_one, 4)
    prepare_factor(f_two, fs_two, 16)
    prepare_factor(f_top, fs_top, 64)

    prepare_weights(w_one, wt)
    for c in range(4):
        for j in range(8):
            at = (j ^ (c % 2)) * 64
            real = fs_one[j, c : c + 1, :] * wt[j]
            imag = fs_one[8 + j, c : c + 1, :] * wt[j]
            k_one[c, at : at + 64, 0:256] = real.astype(BF16)
            k_one[c, at : at + 64, 256:512] = imag.astype(BF16)
            k_one[c, 512 + at : 576 + at, 0:256] = (-imag).astype(BF16)
            k_one[c, 512 + at : 576 + at, 256:512] = real.astype(BF16)

    prepare_weights(w_two, wt)

    @pl.loop(0, 8)
    def _(pair):
        for odd in range(2):
            c = pair * 2 + odd
            for j in range(8):
                at = (j ^ odd) * 64
                k_two[c, at : at + 64, :] = (fs_two[j, pl.ds(c, 1), :] * wt[j]).astype(BF16)
                k_two[c, 512 + at : 576 + at, :] = (fs_two[8 + j, pl.ds(c, 1), :] * wt[j]).astype(BF16)

    prepare_weights(w_top, wt)
    for j in range(8):
        zero = jnp.zeros((64, 256), BF16)
        w_block[0, j, 0:64, :] = wt[j].astype(BF16)
        w_block[0, j, 64:128, :] = zero
        w_block[1, j, 0:64, :] = zero
        w_block[1, j, 64:128, :] = wt[j].astype(BF16)

    rows_copy.wait()
    rows = mask_rows[...].astype(F32).astype(BF16)
    for c in range(16):
        mask_top_x[c] = jnp.dot(
            rows[:, 16 * c : 16 * c + 16], spread_top[...], preferred_element_type=F32
        )

    @pl.loop(0, CHUNKS)
    def _(chunk):
        low = low_lane(N2)
        for c in range(4):
            result = jnp.dot(lhs_one[c], k_one[c], preferred_element_type=F32)
            masks = jnp.dot(
                mask_one_t[pl.ds(chunk * BLOCK, BLOCK), :], spread_one[c], preferred_element_type=F32
            )
            for z in range(2):
                rows = slice(z * N2, z * N2 + N2)
                other = slice((1 - z) * N2, (1 - z) * N2 + N2)
                for m in range(4):
                    lanes = slice(m * 128, m * 128 + 128)
                    lanes_other = slice(512 + m * 128, 640 + m * 128)
                    for t in range(2):
                        a, b = [
                            result[j * N2 : (j + 1) * N2, z * 256 + t * 128 : z * 256 + t * 128 + 128]
                            * masks[j * N2 : (j + 1) * N2, t * 128 : t * 128 + 128]
                            for j in (2 * m, 2 * m + 1)
                        ]
                        b = pltpu.roll(b, 64, 1)
                        even, odd = jnp.where(low, a, b), jnp.where(low, b, a)
                        lhs_two[4 * c + 2 * t, rows, lanes] = even.astype(BF16)
                        lhs_two[4 * c + 2 * t + 1, rows, lanes] = odd.astype(BF16)
                        if z == 1:
                            even, odd = -even, -odd
                        lhs_two[4 * c + 2 * t, other, lanes_other] = even.astype(BF16)
                        lhs_two[4 * c + 2 * t + 1, other, lanes_other] = odd.astype(BF16)

        for c in range(16):
            result = jnp.dot(lhs_two[c], k_two[c], preferred_element_type=F32)
            masks = jnp.dot(mask_two_t[pl.ds(chunk * N2, N2), :], spread_two[c], preferred_element_type=F32)
            for j in range(8):
                at = slice(j * N3, (j + 1) * N3)
                both = [result[z * N2 + j * N3 : z * N2 + (j + 1) * N3] * masks[at] for z in range(2)]
                lhs_top[j, c * ROWS3 : (c + 1) * ROWS3, :] = jnp.concatenate(both, axis=0).astype(BF16)

        for s in range(4):
            half = (s // 2) * 128
            real = [None] * 16
            imag = [None] * 16
            for j in range(8):
                part = jnp.dot(
                    lhs_top[j, :, half : half + 128], w_block[s % 2, j], preferred_element_type=F32
                )
                for g in range(16):
                    re = part[g * ROWS3 : g * ROWS3 + N3]
                    im = part[g * ROWS3 + N3 : (g + 1) * ROWS3]
                    c = 4 * g + s
                    f0 = fs_top[j, c : c + 1, :]
                    f1 = fs_top[8 + j, c : c + 1, :]
                    new_re = f0 * re - f1 * im
                    new_im = f1 * re + f0 * im
                    real[g] = new_re if j == 0 else real[g] + new_re
                    imag[g] = new_im if j == 0 else imag[g] + new_im
            for g in range(16):
                mask = mask_top_x[g, pl.ds(chunk * N3, N3), s * 256 : s * 256 + 256]
                top_out[4 * g + s, 0] = real[g] * mask
                top_out[4 * g + s, 1] = imag[g] * mask

        for i in range(32):
            low = low_lane(N3)
            c0, c1 = order[2 * i], order[2 * i + 1]
            for z in range(2):
                for t in range(2):
                    a = top_out[c0, z, :, t * 128 : t * 128 + 128]
                    b = top_out[c1, z, :, t * 128 : t * 128 + 128]
                    send_buf[chunk, 2 * t * 32 + i, z] = jnp.where(low, a, pltpu.roll(b, 64, 1)).astype(BF16)
                    send_buf[chunk, (2 * t + 1) * 32 + i, z] = jnp.where(
                        low, pltpu.roll(a, 64, 1), b
                    ).astype(BF16)

        @pl.when(chunk == 0)
        def _():
            pl.semaphore_wait(barrier, DEVICES - 1)

        pltpu.make_async_copy(send_buf.at[chunk, me], received.at[:, me, chunk], local_sem).start()
        for offset in offsets():
            to_box, to_cone = target(offset)
            pltpu.make_async_remote_copy(
                src_ref=send_buf.at[chunk, to_box * 32 + to_cone],
                dst_ref=received.at[:, me, chunk],
                send_sem=send_sem,
                recv_sem=recv_sem,
                device_id=(to_box, to_cone),
                device_id_type=MESH,
            ).start()

        @pl.when(chunk + 1 < CHUNKS)
        def _():
            slot = (chunk + 1) % 2
            fetched(slot)
            relay(slot, chunk + 1)

            @pl.when(chunk + 3 < CHUNKS)
            def _():
                fetch(chunk + 3, slot)

    whole = send_buf.at[:, pl.ds(0, DEVICES - 1)]
    pltpu.make_async_copy(send_buf.at[:, 0], send_buf.at[:, 0], local_sem).wait()
    pltpu.make_async_copy(whole, whole, send_sem).wait()
    pltpu.make_async_copy(whole, whole, recv_sem).wait()


def widen(received, top, narrow, wide, in_sem, out_sem):
    part = 1024
    at = [pl.ds(i * part, part) for i in range(8)]
    copies_in = [pltpu.make_async_copy(received.at[a], narrow.at[a], in_sem.at[i]) for i, a in enumerate(at)]
    copies_out = [pltpu.make_async_copy(wide.at[a], top.at[a], out_sem.at[i]) for i, a in enumerate(at)]
    for copy in copies_in:
        copy.start()
    for i, a in enumerate(at):
        copies_in[i].wait()
        wide[a] = narrow[a].astype(F32)
        copies_out[i].start()
    for copy in copies_out:
        copy.wait()


def on_device(
    fine_values, present, mask_one, mask_two, mask_top,
    interp_one, interp_two, interp_top, factor_one, factor_two, factor_top, cone_order,
):
    hbm = pl.BlockSpec(memory_space=pl.ANY)
    received = pl.pallas_call(
        kernel,
        out_shape=jax.ShapeDtypeStruct((2, DEVICES, CHUNKS, N3, 128), BF16),
        in_specs=[hbm] * 11 + [pl.BlockSpec(memory_space=pltpu.SMEM)],
        out_specs=hbm,
        scratch_shapes=[
            pltpu.VMEM((8, B1), jnp.int32),
            pltpu.VMEM((16, B1), jnp.int32),
            pltpu.VMEM((8, 256, 64), BF16),
            pltpu.VMEM((256, 64), F32),
            pltpu.VMEM((64, B1 // 8), jnp.int32),
            pltpu.VMEM((8, 256, 64), BF16),
            pltpu.VMEM((1024, 64), F32),
            pltpu.VMEM((8, 256, 64), BF16),
            pltpu.VMEM((4096, 64), F32),
            pltpu.VMEM((2, 2, BLOCK * 8, 256), BF16),
            pltpu.VMEM((2, 256, 1024), F32),
            pltpu.VMEM((4, BLOCK, 1024), BF16),
            pltpu.VMEM((4, 1024, 512), BF16),
            pltpu.VMEM((16, 2 * N2, 1024), BF16),
            pltpu.VMEM((16, 1024, 256), BF16),
            pltpu.VMEM((8, 16 * ROWS3, 256), BF16),
            pltpu.VMEM((2, 8, 128, 256), BF16),
            pltpu.VMEM((256, 256), BF16),
            pltpu.VMEM((B1, 8), BF16),
            pltpu.VMEM((B1, 16), BF16),
            pltpu.VMEM((B1 // 8, 64), BF16),
            pltpu.VMEM((8, 1024), BF16),
            pltpu.VMEM((4, 16, 256), BF16),
            pltpu.VMEM((16, 64, 256), BF16),
            pltpu.VMEM((16, 1024), BF16),
            pltpu.VMEM((32, 256), jnp.int32),
            pltpu.VMEM((16, 32, 1024), F32),
            pltpu.VMEM((8, 64, 256), F32),
            pltpu.VMEM((16, 4, 256), F32),
            pltpu.VMEM((16, 16, 256), F32),
            pltpu.VMEM((16, 64, 256), F32),
            pltpu.VMEM((64, 2, N3, 256), F32),
            pltpu.VMEM((CHUNKS, DEVICES, 2, N3, 128), BF16),
            pltpu.SemaphoreType.DMA((2,)),
            pltpu.SemaphoreType.DMA,
            pltpu.SemaphoreType.DMA,
            pltpu.SemaphoreType.DMA,
            pltpu.SemaphoreType.DMA,
            pltpu.SemaphoreType.DMA((9,)),
        ],
        compiler_params=pltpu.CompilerParams(
            collective_id=0, has_side_effects=True, vmem_limit_bytes=60 << 20
        ),
        name="levels",
    )(
        fine_values,
        mask_top,
        present.T,
        mask_one.T,
        interp_one.reshape(8, 256, 64),
        factor_one.reshape(-1, 64),
        mask_two.T,
        interp_two.reshape(8, 256, 64),
        factor_two.reshape(-1, 64),
        interp_top.reshape(8, 256, 64),
        factor_top.reshape(-1, 64),
        cone_order,
    )
    top = pl.pallas_call(
        widen,
        out_shape=jax.ShapeDtypeStruct((8192, 128), F32),
        in_specs=[hbm],
        out_specs=hbm,
        scratch_shapes=[
            pltpu.VMEM((8192, 128), BF16),
            pltpu.VMEM((8192, 128), F32),
            pltpu.SemaphoreType.DMA((8,)),
            pltpu.SemaphoreType.DMA((8,)),
        ],
        compiler_params=pltpu.CompilerParams(vmem_limit_bytes=60 << 20),
        name="widen",
    )(received.reshape(8192, 128))
    return top.reshape(2, DEVICES * 32, 128)


def solution(mesh):
    split = P(("box", "cone"), None)
    in_specs = (P(None, ("box", "cone"), None), split, split, split) + (P(),) * 8
    return jax.shard_map(
        on_device,
        mesh=mesh,
        in_specs=in_specs,
        out_specs=P(None, None, ("box", "cone")),
        check_vma=False,
    )
```

```python
import functools

import jax
import jax.numpy as jnp
from jax import lax
from jax.experimental import pallas as pl
from jax.experimental.pallas import tpu as pltpu
from jax.sharding import PartitionSpec as P

F32 = jnp.float32
BF16 = jnp.bfloat16
MESH = pl.DeviceIdType.MESH

DEVICES = 128
B1 = 2048
CHUNKS = 4
BLOCK = B1 // CHUNKS
N2 = BLOCK // 8
N3 = N2 // 8
ROWS3 = 2 * N3


def offsets():
    every = [
        (x, y, z, core) for x in range(4) for y in range(4) for z in range(4) for core in range(2)
    ][1:]
    hops = lambda o: sum(min(v, 4 - v) for v in o[:3])
    order = sorted(range(127), key=lambda i: (i * 77 + 31) % 127)
    return sorted([every[i] for i in order], key=lambda o: -hops(o))


def target(offset):
    box, cone = lax.axis_index("box"), lax.axis_index("cone")
    x = (box // 2) * 2 + cone // 16
    x = (x + offset[0]) % 4
    y = (cone // 4 + offset[1]) % 4
    z = (cone + offset[2]) % 4
    core = (box + offset[3]) % 2
    return (x // 2) * 2 + core, (x % 2) * 16 + y * 4 + z


def prepare_factor(f_ref, scratch, cones):
    for rj in range(16):
        parts = [f_ref[pl.ds(rj * cones * 4 + s, cones, stride=4), :] for s in range(4)]
        scratch[rj] = jnp.concatenate(parts, axis=1)


def prepare_weights(w_ref, scratch):
    row = lax.broadcasted_iota(jnp.int32, (64, 64), 0)
    column = lax.broadcasted_iota(jnp.int32, (64, 64), 1)
    eye = (row == column).astype(BF16)
    for j in range(8):
        scratch[j] = lax.dot_general(
            eye, w_ref[j], (((1,), (1,)), ((), ())), preferred_element_type=F32
        )


def spread(rows, columns, width, first):
    row = lax.broadcasted_iota(jnp.int32, (rows, columns), 0)
    column = lax.broadcasted_iota(jnp.int32, (rows, columns), 1)
    return (row == first + column // width).astype(BF16)


def kernel(
    fine, present, mask_one, mask_two, mask_top, w_one, w_two, w_top, f_one, f_two, f_top, order,
    received,
    fine_buf, here, lhs_one, k_one, lhs_two, k_two, lhs_top, w_block, gather,
    present_t, mask_one_t, mask_two_t, spread_present, spread_one, spread_two, spread_top,
    mask_rows, mask_top_x, wt, fs_one, fs_two, fs_top, top_out, send_buf,
    fine_sem, mask_sem, send_sem, recv_sem, local_sem,
):
    box, cone_index = lax.axis_index("box"), lax.axis_index("cone")
    me = box * 32 + cone_index
    low_lane = lambda rows: lax.broadcasted_iota(jnp.int32, (rows, 128), 1) < 64

    def fetch(chunk, slot):
        part = BLOCK * 8 // 4
        for r in range(2):
            for i in range(4):
                pltpu.make_async_copy(
                    fine.at[r, pl.ds(chunk * (BLOCK * 8) + i * part, part), :],
                    fine_buf.at[slot, r, pl.ds(i * part, part), :],
                    fine_sem.at[slot],
                ).start()

    def fetched(slot):
        pltpu.make_async_copy(fine_buf.at[slot], fine_buf.at[slot], fine_sem.at[slot]).wait()

    fetch(0, 0)
    fetch(1, 1)
    rows_copy = pltpu.make_async_copy(mask_top.at[pl.ds(me * 32, 32)], mask_rows, mask_sem)
    rows_copy.start()

    barrier = pltpu.get_barrier_semaphore()
    for offset in offsets():
        pl.semaphore_signal(barrier, inc=1, device_id=target(offset), device_id_type=MESH)

    row = lax.broadcasted_iota(jnp.int32, (256, 256), 0)
    column = lax.broadcasted_iota(jnp.int32, (256, 256), 1)
    gather[...] = (column == (row % 8) * 32 + (row // 8) % 4 * 8 + row // 32).astype(BF16)
    row = lax.broadcasted_iota(jnp.int32, (BLOCK, BLOCK), 0)
    column = lax.broadcasted_iota(jnp.int32, (BLOCK, BLOCK), 1)
    reorder_one = (column == (row % 8) * 64 + (row // 8) % 8 * 8 + row // 64).astype(BF16)
    row = lax.broadcasted_iota(jnp.int32, (N2, N2), 0)
    column = lax.broadcasted_iota(jnp.int32, (N2, N2), 1)
    reorder_two = (column == (row % 8) * 8 + row // 8).astype(BF16)
    turned = lambda order, mask: lax.dot_general(
        order, mask.astype(F32).astype(BF16), (((1,), (1,)), ((), ())), preferred_element_type=F32
    ).astype(BF16)
    for i in range(CHUNKS):
        at = slice(i * BLOCK, (i + 1) * BLOCK)
        present_t[at, :] = turned(reorder_one, present[:, at])
        mask_one_t[at, :] = turned(reorder_one, mask_one[:, at])
        at = slice(i * N2, (i + 1) * N2)
        mask_two_t[at, :] = turned(reorder_two, mask_two[:, at])
    spread_present[...] = spread(8, 1024, 128, 0)
    for c in range(4):
        spread_one[c] = spread(16, 256, 64, 4 * c)
    for c in range(16):
        spread_two[c] = spread(64, 256, 64, 4 * c)
    spread_top[...] = spread(16, 1024, 64, 0)
    prepare_factor(f_one, fs_one, 4)
    prepare_factor(f_two, fs_two, 16)
    prepare_factor(f_top, fs_top, 64)

    prepare_weights(w_one, wt)
    for c in range(4):
        for j in range(8):
            at = (j ^ (c % 2)) * 64
            real = fs_one[j, c : c + 1, :] * wt[j]
            imag = fs_one[8 + j, c : c + 1, :] * wt[j]
            k_one[c, at : at + 64, 0:256] = real.astype(BF16)
            k_one[c, at : at + 64, 256:512] = imag.astype(BF16)
            k_one[c, 512 + at : 576 + at, 0:256] = (-imag).astype(BF16)
            k_one[c, 512 + at : 576 + at, 256:512] = real.astype(BF16)

    prepare_weights(w_two, wt)

    @pl.loop(0, 8)
    def _(pair):
        for odd in range(2):
            c = pair * 2 + odd
            for j in range(8):
                at = (j ^ odd) * 64
                k_two[c, at : at + 64, :] = (fs_two[j, pl.ds(c, 1), :] * wt[j]).astype(BF16)
                k_two[c, 512 + at : 576 + at, :] = (fs_two[8 + j, pl.ds(c, 1), :] * wt[j]).astype(BF16)

    prepare_weights(w_top, wt)
    for j in range(8):
        zero = jnp.zeros((64, 256), BF16)
        w_block[0, j, 0:64, :] = wt[j].astype(BF16)
        w_block[0, j, 64:128, :] = zero
        w_block[1, j, 0:64, :] = zero
        w_block[1, j, 64:128, :] = wt[j].astype(BF16)

    rows_copy.wait()
    rows = mask_rows[...].astype(F32).astype(BF16)
    for c in range(16):
        mask_top_x[c] = jnp.dot(
            rows[:, 16 * c : 16 * c + 16], spread_top[...], preferred_element_type=F32
        )

    def relay(slot, chunk):
        low = low_lane(16)
        for half in range(2):
            at = pl.ds(chunk * BLOCK + half * 256, 256)
            here[half] = jnp.dot(present_t[at, :], spread_present[...], preferred_element_type=F32)
            for pair in range(4):
                for r in range(2):
                    picked = []
                    for j2 in (2 * pair, 2 * pair + 1):
                        rows = [
                            fine_buf[slot, r, (8 * p + j2) * 64 + half * 32 : (8 * p + j2) * 64 + half * 32 + 32, :]
                            for p in range(8)
                        ]
                        picked.append(
                            jnp.dot(gather[...], jnp.concatenate(rows, axis=0), preferred_element_type=F32)
                        )
                    for j1 in range(4):
                        at = j1 * 64 + pair * 16
                        to = half * 256 + at
                        for m in range(4):
                            lanes = slice(r * 512 + m * 128, r * 512 + m * 128 + 128)
                            for t in range(2):
                                a, b = [
                                    jnp.concatenate(
                                        [
                                            part[j * 32 + j1 * 8 : j * 32 + j1 * 8 + 8, t * 128 : t * 128 + 128]
                                            for part in picked
                                        ],
                                        axis=0,
                                    )
                                    * here[half, at : at + 16, j * 128 : j * 128 + 128]
                                    for j in (2 * m, 2 * m + 1)
                                ]
                                b = pltpu.roll(b, 64, 1)
                                lhs_one[2 * t, to : to + 16, lanes] = jnp.where(low, a, b).astype(BF16)
                                lhs_one[2 * t + 1, to : to + 16, lanes] = jnp.where(low, b, a).astype(BF16)

    @pl.loop(0, CHUNKS)
    def _(chunk):
        slot = chunk % 2
        fetched(slot)
        relay(slot, chunk)

        @pl.when(chunk + 2 < CHUNKS)
        def _():
            fetch(chunk + 2, slot)

        low = low_lane(N2)
        for c in range(4):
            result = jnp.dot(lhs_one[c], k_one[c], preferred_element_type=F32)
            masks = jnp.dot(
                mask_one_t[pl.ds(chunk * BLOCK, BLOCK), :], spread_one[c], preferred_element_type=F32
            )
            for z in range(2):
                rows = slice(z * N2, z * N2 + N2)
                other = slice((1 - z) * N2, (1 - z) * N2 + N2)
                for m in range(4):
                    lanes = slice(m * 128, m * 128 + 128)
                    lanes_other = slice(512 + m * 128, 640 + m * 128)
                    for t in range(2):
                        a, b = [
                            result[j * N2 : (j + 1) * N2, z * 256 + t * 128 : z * 256 + t * 128 + 128]
                            * masks[j * N2 : (j + 1) * N2, t * 128 : t * 128 + 128]
                            for j in (2 * m, 2 * m + 1)
                        ]
                        b = pltpu.roll(b, 64, 1)
                        even, odd = jnp.where(low, a, b), jnp.where(low, b, a)
                        lhs_two[4 * c + 2 * t, rows, lanes] = even.astype(BF16)
                        lhs_two[4 * c + 2 * t + 1, rows, lanes] = odd.astype(BF16)
                        if z == 1:
                            even, odd = -even, -odd
                        lhs_two[4 * c + 2 * t, other, lanes_other] = even.astype(BF16)
                        lhs_two[4 * c + 2 * t + 1, other, lanes_other] = odd.astype(BF16)

        for c in range(16):
            result = jnp.dot(lhs_two[c], k_two[c], preferred_element_type=F32)
            masks = jnp.dot(mask_two_t[pl.ds(chunk * N2, N2), :], spread_two[c], preferred_element_type=F32)
            for j in range(8):
                at = slice(j * N3, (j + 1) * N3)
                both = [result[z * N2 + j * N3 : z * N2 + (j + 1) * N3] * masks[at] for z in range(2)]
                lhs_top[j, c * ROWS3 : (c + 1) * ROWS3, :] = jnp.concatenate(both, axis=0).astype(BF16)

        for s in range(4):
            half = (s // 2) * 128
            real = [None] * 16
            imag = [None] * 16
            for j in range(8):
                part = jnp.dot(
                    lhs_top[j, :, half : half + 128], w_block[s % 2, j], preferred_element_type=F32
                )
                for g in range(16):
                    re = part[g * ROWS3 : g * ROWS3 + N3]
                    im = part[g * ROWS3 + N3 : (g + 1) * ROWS3]
                    c = 4 * g + s
                    f0 = fs_top[j, c : c + 1, :]
                    f1 = fs_top[8 + j, c : c + 1, :]
                    new_re = f0 * re - f1 * im
                    new_im = f1 * re + f0 * im
                    real[g] = new_re if j == 0 else real[g] + new_re
                    imag[g] = new_im if j == 0 else imag[g] + new_im
            for g in range(16):
                mask = mask_top_x[g, pl.ds(chunk * N3, N3), s * 256 : s * 256 + 256]
                top_out[4 * g + s, 0] = real[g] * mask
                top_out[4 * g + s, 1] = imag[g] * mask

        @pl.loop(0, 32, unroll=32)
        def _(i):
            low = low_lane(N3)
            c0, c1 = order[2 * i], order[2 * i + 1]
            for z in range(2):
                for t in range(2):
                    a = top_out[c0, z, :, t * 128 : t * 128 + 128]
                    b = top_out[c1, z, :, t * 128 : t * 128 + 128]
                    send_buf[chunk, 2 * t * 32 + i, z] = jnp.where(low, a, pltpu.roll(b, 64, 1)).astype(BF16)
                    send_buf[chunk, (2 * t + 1) * 32 + i, z] = jnp.where(
                        low, pltpu.roll(a, 64, 1), b
                    ).astype(BF16)

        @pl.when(chunk == 0)
        def _():
            pl.semaphore_wait(barrier, DEVICES - 1)

        pltpu.make_async_copy(send_buf.at[chunk, me], received.at[:, me, chunk], local_sem).start()
        for offset in offsets():
            to_box, to_cone = target(offset)
            pltpu.make_async_remote_copy(
                src_ref=send_buf.at[chunk, to_box * 32 + to_cone],
                dst_ref=received.at[:, me, chunk],
                send_sem=send_sem,
                recv_sem=recv_sem,
                device_id=(to_box, to_cone),
                device_id_type=MESH,
            ).start()

    whole = send_buf.at[:, pl.ds(0, DEVICES - 1)]
    pltpu.make_async_copy(send_buf.at[:, 0], send_buf.at[:, 0], local_sem).wait()
    pltpu.make_async_copy(whole, whole, send_sem).wait()
    pltpu.make_async_copy(whole, whole, recv_sem).wait()


def widen(received, top, narrow, wide, in_sem, out_sem):
    part = 1024
    at = [pl.ds(i * part, part) for i in range(8)]
    copies_in = [pltpu.make_async_copy(received.at[a], narrow.at[a], in_sem.at[i]) for i, a in enumerate(at)]
    copies_out = [pltpu.make_async_copy(wide.at[a], top.at[a], out_sem.at[i]) for i, a in enumerate(at)]
    for copy in copies_in:
        copy.start()
    for i, a in enumerate(at):
        copies_in[i].wait()
        wide[a] = narrow[a].astype(F32)
        copies_out[i].start()
    for copy in copies_out:
        copy.wait()


def on_device(
    fine_values, present, mask_one, mask_two, mask_top,
    interp_one, interp_two, interp_top, factor_one, factor_two, factor_top, cone_order,
):
    vmem = pl.BlockSpec(memory_space=pltpu.VMEM)
    hbm = pl.BlockSpec(memory_space=pl.ANY)
    received = pl.pallas_call(
        kernel,
        out_shape=jax.ShapeDtypeStruct((2, DEVICES, CHUNKS, N3, 128), BF16),
        in_specs=[hbm, vmem, vmem, vmem, hbm] + [vmem] * 6 + [pl.BlockSpec(memory_space=pltpu.SMEM)],
        out_specs=hbm,
        scratch_shapes=[
            pltpu.VMEM((2, 2, BLOCK * 8, 256), BF16),
            pltpu.VMEM((2, 256, 1024), F32),
            pltpu.VMEM((4, BLOCK, 1024), BF16),
            pltpu.VMEM((4, 1024, 512), BF16),
            pltpu.VMEM((16, 2 * N2, 1024), BF16),
            pltpu.VMEM((16, 1024, 256), BF16),
            pltpu.VMEM((8, 16 * ROWS3, 256), BF16),
            pltpu.VMEM((2, 8, 128, 256), BF16),
            pltpu.VMEM((256, 256), BF16),
            pltpu.VMEM((B1, 8), BF16),
            pltpu.VMEM((B1, 16), BF16),
            pltpu.VMEM((B1 // 8, 64), BF16),
            pltpu.VMEM((8, 1024), BF16),
            pltpu.VMEM((4, 16, 256), BF16),
            pltpu.VMEM((16, 64, 256), BF16),
            pltpu.VMEM((16, 1024), BF16),
            pltpu.VMEM((32, 256), jnp.int32),
            pltpu.VMEM((16, 32, 1024), F32),
            pltpu.VMEM((8, 64, 256), F32),
            pltpu.VMEM((16, 4, 256), F32),
            pltpu.VMEM((16, 16, 256), F32),
            pltpu.VMEM((16, 64, 256), F32),
            pltpu.VMEM((64, 2, N3, 256), F32),
            pltpu.VMEM((CHUNKS, DEVICES, 2, N3, 128), BF16),
            pltpu.SemaphoreType.DMA((2,)),
            pltpu.SemaphoreType.DMA,
            pltpu.SemaphoreType.DMA,
            pltpu.SemaphoreType.DMA,
            pltpu.SemaphoreType.DMA,
        ],
        compiler_params=pltpu.CompilerParams(
            collective_id=0, has_side_effects=True, vmem_limit_bytes=60 << 20
        ),
        name="levels",
    )(
        fine_values,
        present.T,
        mask_one.T,
        mask_two.T,
        mask_top,
        interp_one.reshape(8, 256, 64),
        interp_two.reshape(8, 256, 64),
        interp_top.reshape(8, 256, 64),
        factor_one.reshape(-1, 64),
        factor_two.reshape(-1, 64),
        factor_top.reshape(-1, 64),
        cone_order,
    )
    top = pl.pallas_call(
        widen,
        out_shape=jax.ShapeDtypeStruct((8192, 128), F32),
        in_specs=[hbm],
        out_specs=hbm,
        scratch_shapes=[
            pltpu.VMEM((8192, 128), BF16),
            pltpu.VMEM((8192, 128), F32),
            pltpu.SemaphoreType.DMA((8,)),
            pltpu.SemaphoreType.DMA((8,)),
        ],
        compiler_params=pltpu.CompilerParams(vmem_limit_bytes=60 << 20),
        name="widen",
    )(received.reshape(8192, 128))
    return top.reshape(2, DEVICES * 32, 128)


def solution(mesh):
    split = P(("box", "cone"), None)
    in_specs = (P(None, ("box", "cone"), None), split, split, split) + (P(),) * 8
    return jax.shard_map(
        on_device,
        mesh=mesh,
        in_specs=in_specs,
        out_specs=P(None, None, ("box", "cone")),
        check_vma=False,
    )
```
